256 devices in a mesh: stn: 32 (over z, x), tm: 8 (over y, core).
Axes of the slice: x: 4, y: 4, z: 8, core: 2. Of those that a mesh axis runs over, the one named last changes fastest.
Arguments:
- streams: bfloat16 [2, 32, 4194304], P(None, 'stn', 'tm'), may hold values from -6 to 6
- sample_delays: int32 [32], P('stn'), may hold values from 0 to 2048, as said below
- fringe_rates: int32 [32], P('stn'), may hold values from -32768 to 32768
Outputs:
- visibilities: float32 [2, 32, 32, 4096], P(None, 'tm', None, 'stn')
- auto_spectra: float32 [32, 4096], P('tm', 'stn')
The draws below stay inside these ranges and needn't reach their ends.
Inputs may be any that keep to these rules, and one draw needn't show every extreme that they name: `sample_delays`: one station's delay is exactly 2048.
All inputs are finite; a program needn't handle non-finite values.
Results may differ from the reference program's by a relative error of at most 0.0082.
Values may be sent and summed in bfloat16 or wider, within the bound.
A program may use at most 64 MiB of HBM per device.

```python
import math
import jax
import jax.numpy as jnp
from jax import lax

FAC_A = 16
FAC_B = 256
NCH = 4096
MAXD = 2048
STATIONS = 32
FRAMES_DEV = 128
FRAMES = 1024
TIME = 4194304
N_TM = 8


def draw_sample_delays(key, part):
    key = jax.random.fold_in(key, 11)
    values = jax.random.randint(key, (STATIONS,), 0, MAXD + 1, dtype=jnp.int32)
    chosen = jax.random.randint(jax.random.fold_in(key, 12), (), 0, STATIONS, dtype=jnp.int32)
    return jnp.where(jnp.arange(STATIONS, dtype=jnp.int32) == chosen, MAXD, values).astype(jnp.int32)


def plant(drawn, key, least, high):
    dims = drawn.shape
    place = [jax.random.randint(jax.random.fold_in(key, axis), (), 0, dims[axis]) for axis in range(len(dims))]
    drawn = drawn.at[tuple(place)].set(least)
    longest = dims.index(max(dims))
    place[longest] = (place[longest] + 1) % dims[longest]
    return drawn.at[tuple(place)].set(high)


def levels(own_key, extent, cuts, smallest, top_value):
    level = 1.0
    for axis_at, shards_of in cuts:
        steps = jax.random.uniform(jax.random.fold_in(jax.random.fold_in(own_key, 6), axis_at), (shards_of,), jnp.float32, smallest / len(cuts), top_value / len(cuts))
        level = level * jnp.repeat(jnp.exp(steps), extent[axis_at] // shards_of).reshape((-1,) + (1,) * (len(extent) - 1 - axis_at))
    return level


def scatter_about(own_key, shape, width, limit, cuts=(), kind=jnp.bfloat16):
    entries = jax.random.normal(own_key, shape, jnp.float32) * width
    if len(cuts) > 0:
        entries = levels(own_key, shape, cuts, -0.22, 0.18) * entries
    return jnp.clip(entries, min=-limit, max=limit).astype(kind)


def setup_inputs(seed: int = 0) -> dict:
    seeds = jax.random.split(jax.random.key(seed), 4)
    return {
        "streams": scatter_about(seeds[0], (2, STATIONS, TIME), 1.0, 6.0, ((1, 32), (2, 8))),
        "sample_delays": draw_sample_delays(jax.random.fold_in(seeds[3], 71), 0),
        "fringe_rates": plant(jax.random.randint(seeds[2], (STATIONS,), -32768, 32769), jax.random.fold_in(seeds[2], 1), -32768, 32768).astype(jnp.int32),
    }


two_pi = 2.0 * math.pi
turn_split = 1024
full_turn = 1048576.0

def phase_turns(rate_col, times):
    upper = times // turn_split
    lower = times % turn_split
    high = jnp.mod(rate_col * upper, turn_split)
    return jnp.mod(high * turn_split + rate_col * lower, turn_split * turn_split)

def dft_tables():
    first_idx = jnp.arange(FAC_A, dtype=jnp.int32)
    second_idx = jnp.arange(FAC_B, dtype=jnp.int32)
    angle_first = two_pi * (jnp.mod(first_idx[:, None] * first_idx[None, :], FAC_A).astype(jnp.float32) / FAC_A)
    angle_twiddle = two_pi * (jnp.mod(first_idx[:, None] * second_idx[None, :], NCH).astype(jnp.float32) / NCH)
    angle_second = two_pi * (jnp.mod(second_idx[:, None] * second_idx[None, :], FAC_B).astype(jnp.float32) / FAC_B)
    norm_scale = 1.0 / math.sqrt(NCH)
    return (jnp.cos(angle_first).astype(jnp.bfloat16), jnp.sin(angle_first).astype(jnp.bfloat16), jnp.cos(angle_twiddle) * norm_scale, jnp.sin(angle_twiddle) * norm_scale, jnp.cos(angle_second).astype(jnp.bfloat16), jnp.sin(angle_second).astype(jnp.bfloat16))

def rotate(real_in, imag_in, rate_vec, times):
    turns = phase_turns(rate_vec[:, None], times[None, :])
    angle = two_pi * turns.astype(jnp.float32) / full_turn
    cosine = jnp.cos(angle)
    sine = jnp.sin(angle)
    real_out = (real_in * cosine + imag_in * sine).astype(jnp.bfloat16)
    imag_out = (imag_in * cosine - real_in * sine).astype(jnp.bfloat16)
    return (real_out, imag_out)

def first_section(data, table):
    return jnp.einsum('sfan,ak->sfkn', data.astype(jnp.float32), table.astype(jnp.float32))

def second_section(data, table):
    return jnp.einsum('sfkn,nm->sfmk', data.astype(jnp.float32), table.astype(jnp.float32))

def channelize(real_in, imag_in, tables):
    cos_first, sin_first, cos_twid, sin_twid, cos_second, sin_second = tables
    stations, length = real_in.shape
    frames = length // NCH
    real_frames = real_in.reshape(stations, frames, FAC_A, FAC_B)
    imag_frames = imag_in.reshape(stations, frames, FAC_A, FAC_B)
    part_real = first_section(real_frames, cos_first) + first_section(imag_frames, sin_first)
    part_imag = first_section(imag_frames, cos_first) - first_section(real_frames, sin_first)
    turn_real = (part_real * cos_twid + part_imag * sin_twid).astype(jnp.bfloat16)
    turn_imag = (part_imag * cos_twid - part_real * sin_twid).astype(jnp.bfloat16)
    spec_real = second_section(turn_real, cos_second) + second_section(turn_imag, sin_second)
    spec_imag = second_section(turn_imag, cos_second) - second_section(turn_real, sin_second)
    return (spec_real.reshape(stations, frames, NCH).astype(jnp.bfloat16), spec_imag.reshape(stations, frames, NCH).astype(jnp.bfloat16))

def correlate(spec_real, spec_imag):
    left_real = spec_real.astype(jnp.float32)
    left_imag = spec_imag.astype(jnp.float32)
    corr_real = jnp.einsum('sfc,tfc->stc', left_real, left_real) + jnp.einsum('sfc,tfc->stc', left_imag, left_imag)
    corr_imag = jnp.einsum('sfc,tfc->stc', left_imag, left_real) - jnp.einsum('sfc,tfc->stc', left_real, left_imag)
    return (corr_real, corr_imag)

def reference(streams, sample_delays, fringe_rates):
    slice_len = FRAMES_DEV * NCH
    extended = jnp.concatenate([streams, jnp.zeros((2, STATIONS, MAXD), streams.dtype)], axis=2)
    tables = dft_tables()

    def one_slice(block_index, carry):
        start = (block_index * slice_len).astype(jnp.int32)
        pieces = jax.vmap(lambda stream_row, shift_by: lax.dynamic_slice_in_dim(stream_row, start + shift_by, slice_len, 1), in_axes=(1, 0), out_axes=1)(extended, sample_delays.astype(jnp.int32))
        times = start + jnp.arange(slice_len, dtype=jnp.int32)
        real_rot, imag_rot = rotate(pieces[0].astype(jnp.float32), pieces[1].astype(jnp.float32), fringe_rates, times)
        spec_real, spec_imag = channelize(real_rot, imag_rot, tables)
        corr_real, corr_imag = correlate(spec_real, spec_imag)
        return (carry[0] + corr_real, carry[1] + corr_imag)
    zeros_init = jnp.zeros((STATIONS, STATIONS, NCH), jnp.float32)
    corr_real, corr_imag = lax.fori_loop(0, N_TM, one_slice, (zeros_init, zeros_init))
    identity = jnp.eye(STATIONS, dtype=jnp.float32)
    off_diag = (1.0 - identity)[:, :, None]
    inv_root = 1.0 / math.sqrt(FRAMES)
    visibilities = jnp.stack([corr_real * off_diag * inv_root, corr_imag * off_diag * inv_root])
    auto_spectra = lax.optimization_barrier(jnp.sum(corr_real * identity[:, :, None], axis=1)) / FRAMES
    return (visibilities, auto_spectra)
```

```python
import functools
import math

import jax
import jax.numpy as jnp
from jax import lax
from jax.experimental import pallas as pl
from jax.experimental.pallas import tpu as pltpu
from jax.sharding import PartitionSpec as P

MESH = pl.DeviceIdType.MESH

LANES = 128
FIRST = 32
FRAMES_DEV = 128
STATIONS = 32
N_TM = 8
ROWS = 2 * FIRST * FRAMES_DEV
HALO = 32
TURN = 20
CHUNKS = (4, 4, 4, 4)
PAIRS = FIRST // 2
SIN = (1.0, -1 / 6, 1 / 120, -1 / 5040, 1 / 362880, -1 / 39916800, 1 / 6227020800)


def iota(shape, axis):
    return lax.broadcasted_iota(jnp.int32, shape, axis)


def cos_turns(phase):
    wrapped = phase & ((1 << TURN) - 1)
    folded = jnp.abs(wrapped - (1 << (TURN - 1)))
    w = (folded - (1 << (TURN - 2))).astype(jnp.float32) * (2.0 * math.pi / (1 << TURN))
    square = w * w
    total = jnp.full_like(w, SIN[-1])
    for coefficient in SIN[-2::-1]:
        total = total * square + coefficient
    return total * w


def sin_turns(phase):
    return cos_turns(phase - (1 << (TURN - 2)))


def nt_dot(left, right):
    return lax.dot_general(left, right, (((1,), (1,)), ((), ())), preferred_element_type=jnp.float32)


def kernel(
    delay_ref, rate_ref, x_ref, vis_ref, auto_ref,
    xb, first_ref, second_ref, perm_ref, twid_ref, frame_ref, turned_ref,
    tx, rx, rs_tx, rs_rx, acc_ref,
    load_sem, halo_sems, tx_sems, rx_sems, rs_tx_sems, rs_rx_sems,
):
    me = lax.axis_index("stn")
    tm = lax.axis_index("tm")
    barrier = pltpu.get_barrier_semaphore()

    def greet_stn(k, carry):
        pl.semaphore_signal(barrier, inc=1, device_id={"stn": lax.rem(me + k, STATIONS)}, device_id_type=MESH)
        return carry

    def greet_tm(k, carry):
        pl.semaphore_signal(barrier, inc=1, device_id={"tm": lax.rem(tm + k, N_TM)}, device_id_type=MESH)
        return carry

    lax.fori_loop(1, STATIONS, greet_stn, 0)
    lax.fori_loop(1, N_TM, greet_tm, 0)

    load = pltpu.make_async_copy(x_ref, xb.at[pl.ds(0, ROWS)], load_sem)
    load.start()
    xb[pl.ds(ROWS + HALO, 128 - HALO), :] = jnp.zeros((128 - HALO, LANES), jnp.bfloat16)

    @pl.when(tm == N_TM - 1)
    def _():
        xb[pl.ds(ROWS, HALO), :] = jnp.zeros((HALO, LANES), jnp.bfloat16)

    delay = delay_ref[0]
    rate = rate_ref[0]
    whole = delay >> 7
    part = delay & (LANES - 1)

    rows = iota((2 * FIRST, LANES), 0)
    lanes = iota((2 * FIRST, LANES), 1)
    k1 = rows & (FIRST - 1)
    for extra in range(2):
        shift = 2 * (whole + extra)
        j = ((lanes - shift) & 63) >> 1
        comp_in = lanes & 1
        comp_out = rows >> 5
        quarter = (comp_out - comp_in) * (1 << (TURN - 2))
        base = cos_turns(k1 * j * (1 << 15) + rate * 128 * j + quarter)
        base = base.reshape(2 * FIRST, 1, LANES)
        frame = iota((1, 8, LANES), 1)
        lane = iota((1, 8, LANES), 2)
        for v in range(5):
            hit = ((lane + (128 * v - shift)) >> 6) == frame
            block = jnp.where(hit, base, 0.0).reshape(2 * FIRST * 8, LANES)
            first_ref[:, pl.ds(extra * 640 + v * 128, 128)] = block.astype(jnp.bfloat16)

    k1 = iota((FIRST, LANES), 0)
    sample = (iota((FIRST, LANES), 1) - part) & (LANES - 1)
    phase = sample * k1 * 256 + rate * sample
    scale = 1.0 / 64.0
    twid_ref[0] = cos_turns(phase) * scale
    twid_ref[1] = sin_turns(phase) * scale
    start = tm * (FRAMES_DEV * 4096) + iota((FRAMES_DEV, LANES), 0) * 4096
    phase = rate * start
    frame_ref[0] = cos_turns(phase)
    frame_ref[1] = sin_turns(phase)

    row = iota((256, LANES), 0)
    sample = (iota((256, LANES), 1) - part) & (LANES - 1)
    k2 = (row >> 3) * 4 + (row & 3)
    phase = sample * k2 * (1 << 13)
    comp_out = (row >> 2) & 1
    for comp_in in range(2):
        quarter = (comp_out - comp_in) * (1 << (TURN - 2))
        second_ref[:, pl.ds(comp_in * LANES, LANES)] = cos_turns(phase + quarter).astype(jnp.bfloat16)

    out_row = iota((256, 256), 0)
    in_row = iota((256, 256), 1)
    channel = out_row >> 5
    source = (out_row & 15) * 16 + (channel >> 2) * 8 + ((out_row >> 4) & 1) * 4 + (channel & 3)
    perm_ref[...] = jnp.where(in_row == source, 1.0, 0.0).astype(jnp.bfloat16)

    pl.semaphore_wait(barrier, STATIONS - 1 + N_TM - 1)

    def halo(target):
        return pltpu.make_async_remote_copy(
            src_ref=x_ref.at[pl.ds(0, HALO)],
            dst_ref=xb.at[pl.ds(ROWS, HALO)],
            send_sem=halo_sems.at[0],
            recv_sem=halo_sems.at[1],
            device_id={"tm": target},
            device_id_type=MESH,
        )

    @pl.when(tm > 0)
    def _():
        halo(tm - 1).start()

    load.wait()

    lane_of = iota((1, 2 * LANES), 1) & (LANES - 1)
    upper = jnp.where(lane_of >= part, 1.0, 0.0).astype(jnp.bfloat16)
    lower = jnp.where(lane_of < part, 1.0, 0.0).astype(jnp.bfloat16)

    def first_stage(group, carry):
        base = pl.multiple_of(group * 1024, 1024)
        data = jnp.concatenate([xb[pl.ds(base, 640), :], xb[pl.ds(base + 512, 640), :]], axis=1)
        partial = jnp.dot(first_ref[:, pl.ds(0, 640)], data * upper, preferred_element_type=jnp.float32)
        partial += jnp.dot(first_ref[:, pl.ds(640, 640)], data * lower, preferred_element_type=jnp.float32)
        tc = twid_ref[0].reshape(FIRST, 1, LANES)
        ts = twid_ref[1].reshape(FIRST, 1, LANES)
        parts = []
        for half in range(2):
            at = pl.multiple_of(group * 16 + half * 8, 8)
            pc = frame_ref[0, pl.ds(at, 8), :].reshape(1, 8, LANES)
            ps = frame_ref[1, pl.ds(at, 8), :].reshape(1, 8, LANES)
            wc = tc * pc - ts * ps
            ws = ts * pc + tc * ps
            real = partial[:256, half * 128 : half * 128 + 128].reshape(FIRST, 8, LANES)
            imag = partial[256:, half * 128 : half * 128 + 128].reshape(FIRST, 8, LANES)
            parts.append((real * wc + imag * ws, imag * wc - real * ws))
        at = pl.multiple_of(group * 16, 16)
        for comp in range(2):
            both = jnp.concatenate([parts[0][comp], parts[1][comp]], axis=1)
            turned_ref[:, pl.ds(at, 16), pl.ds(comp * 128, 128)] = both.astype(jnp.bfloat16)
        return carry

    lax.fori_loop(0, 7, first_stage, 0)

    @pl.when(tm < N_TM - 1)
    def _():
        halo(tm).wait_recv()

    first_stage(7, 0)

    def second_stage(kp, carry):
        data = turned_ref[pl.ds(2 * kp, 2)].reshape(256, 256)
        spec = nt_dot(second_ref[...], data)
        even = spec[:, :128].reshape(32, 8, 128)
        odd = spec[:, 128:].reshape(32, 8, 128)
        tx[:, kp] = jnp.concatenate([even, odd], axis=1).astype(jnp.bfloat16)
        return carry

    def to_owner(at, count, index, owner):
        return pltpu.make_async_remote_copy(
            src_ref=tx.at[owner, pl.ds(at, count)],
            dst_ref=rx.at[me, pl.ds(at, count)],
            send_sem=tx_sems.at[index],
            recv_sem=rx_sems.at[index],
            device_id={"stn": owner},
            device_id_type=MESH,
        )

    def to_row_owner(at, count, index, owner):
        return pltpu.make_async_remote_copy(
            src_ref=rs_tx.at[owner, pl.ds(at, count)],
            dst_ref=rs_rx.at[tm, pl.ds(at, count)],
            send_sem=rs_tx_sems.at[index],
            recv_sem=rs_rx_sems.at[index],
            device_id={"tm": owner},
            device_id_type=MESH,
        )

    starts = [sum(CHUNKS[:i]) for i in range(len(CHUNKS))]
    for index, (at, count) in enumerate(zip(starts, CHUNKS)):
        lax.fori_loop(at, at + count, second_stage, 0)

        def send(k, carry, at=at, count=count, index=index):
            to_owner(at, count, index, lax.rem(me + k, STATIONS)).start()
            return carry

        lax.fori_loop(1, STATIONS, send, 0)
        pltpu.make_async_copy(
            tx.at[me, pl.ds(at, count)], rx.at[me, pl.ds(at, count)], rx_sems.at[index]
        ).start()

    lane_group = iota((1, LANES), 1) >> 5
    low_rows = iota((1, 8, LANES), 1) < 4

    def correlate(pair, carry):
        halves = []
        for half in range(2):
            data = [rx[pl.ds(16 * half, 16), 2 * pair + i].reshape(256, LANES) for i in range(2)]
            moved = jnp.dot(perm_ref[...], jnp.concatenate(data, axis=1), preferred_element_type=jnp.float32)
            halves.append(moved.astype(jnp.bfloat16).reshape(8, 2, 16, 256))
        for i in range(2):
            cut = slice(128 * i, 128 * i + 128)
            real = jnp.concatenate([halves[0][:, 0, :, cut], halves[1][:, 0, :, cut]], axis=1)
            imag = jnp.concatenate([halves[0][:, 1, :, cut], halves[1][:, 1, :, cut]], axis=1)
            plain = jnp.concatenate([real, imag], axis=2)
            crossed = jnp.concatenate([imag, -real], axis=2)
            both = jnp.concatenate([plain, crossed], axis=1)
            for quad in range(2):
                right = plain[4 * quad : 4 * quad + 4].reshape(128, 256)
                left = both[4 * quad : 4 * quad + 4].reshape(256, 256)
                product = nt_dot(left, right).reshape(4, 64, LANES)
                kept = product[0]
                for e in range(1, 4):
                    kept = jnp.where(lane_group == e, product[e], kept)
                kept = kept.reshape(2, 4, 8, LANES)
                turned = pltpu.roll(kept.reshape(8, 8, LANES), 4, 1).reshape(2, 4, 8, LANES)
                even = jnp.where(low_rows, kept[0], turned[1])
                odd = jnp.where(low_rows, turned[0], kept[1])
                mixed = jnp.concatenate([even.reshape(4, 1, 8, LANES), odd.reshape(4, 1, 8, LANES)], axis=1)
                rs_tx[:, 2 * pair + i, quad] = mixed.reshape(N_TM, 8, LANES)
        return carry

    for index, (at, count) in enumerate(zip(starts, CHUNKS)):
        arrived = rx.at[:, pl.ds(at, count)]
        pltpu.make_async_copy(arrived, arrived, rx_sems.at[index]).wait()
        lax.fori_loop(at // 2, (at + count) // 2, correlate, 0)

        def send(k, carry, at=at, count=count, index=index):
            to_row_owner(at, count, index, lax.rem(tm + k, N_TM)).start()
            return carry

        lax.fori_loop(1, N_TM, send, 0)
        pltpu.make_async_copy(
            rs_tx.at[tm, pl.ds(at, count)], rs_rx.at[tm, pl.ds(at, count)], rs_rx_sems.at[index]
        ).start()

    for index, (at, count) in enumerate(zip(starts, CHUNKS)):
        arrived = rs_rx.at[:, pl.ds(at, count)]
        pltpu.make_async_copy(arrived, arrived, rs_rx_sems.at[index]).wait()
        total = rs_rx[0, pl.ds(at, count)]
        for source in range(1, N_TM):
            total = total + rs_rx[source, pl.ds(at, count)]
        acc_ref[pl.ds(2 * at, 2 * count)] = total.reshape(2 * count, 8, LANES)

    lane_group = iota((32, LANES), 1) >> 5
    station = iota((32, LANES), 0)
    for comp in range(2):
        stacked = jnp.concatenate([acc_ref[:, 4 * comp + r, :] for r in range(4)], axis=0)
        flipped = stacked.T.reshape(4, 32, LANES)
        for r in range(4):
            block = jnp.zeros((32, LANES), jnp.float32)
            for k2 in range(4):
                shift = (32 * (k2 - r)) % 128
                piece = flipped[k2] if shift == 0 else pltpu.roll(flipped[k2], shift, 1)
                block = jnp.where(lane_group == k2, piece, block)
            diagonal = station == 4 * tm + r
            vis_ref[4 * comp + r] = jnp.where(diagonal, 0.0, block * (1.0 / 32.0))
            if comp == 0:
                own = jnp.sum(jnp.where(diagonal, block, 0.0), axis=0, keepdims=True)
                auto_ref[pl.ds(r, 1), :] = own * (1.0 / 1024.0)

    for index, (at, count) in enumerate(zip(starts, CHUNKS)):
        sent = tx.at[pl.ds(0, STATIONS - 1), pl.ds(at, count)]
        pltpu.make_async_copy(sent, sent, tx_sems.at[index]).wait()
        sent = rs_tx.at[pl.ds(0, N_TM - 1), pl.ds(at, count)]
        pltpu.make_async_copy(sent, sent, rs_tx_sems.at[index]).wait()

    @pl.when(tm > 0)
    def _():
        halo(tm).wait_send()


def per_device(streams, sample_delays, fringe_rates):
    data = streams.reshape(2, ROWS // 2, LANES).transpose(1, 0, 2).reshape(ROWS, LANES)
    chunks = len(CHUNKS)
    vis, auto = pl.pallas_call(
        kernel,
        out_shape=(
            jax.ShapeDtypeStruct((8, STATIONS, LANES), jnp.float32),
            jax.ShapeDtypeStruct((4, LANES), jnp.float32),
        ),
        in_specs=[
            pl.BlockSpec(memory_space=pltpu.SMEM),
            pl.BlockSpec(memory_space=pltpu.SMEM),
            pl.BlockSpec(memory_space=pl.ANY),
        ],
        out_specs=(pl.BlockSpec(memory_space=pltpu.VMEM), pl.BlockSpec(memory_space=pltpu.VMEM)),
        scratch_shapes=[
            pltpu.VMEM((ROWS + 128, LANES), jnp.bfloat16),
            pltpu.VMEM((512, 1280), jnp.bfloat16),
            pltpu.VMEM((256, 256), jnp.bfloat16),
            pltpu.VMEM((256, 256), jnp.bfloat16),
            pltpu.VMEM((2, FIRST, LANES), jnp.float32),
            pltpu.VMEM((2, FRAMES_DEV, LANES), jnp.float32),
            pltpu.VMEM((FIRST, FRAMES_DEV, 256), jnp.bfloat16),
            pltpu.VMEM((STATIONS, PAIRS, 16, LANES), jnp.bfloat16),
            pltpu.VMEM((STATIONS, PAIRS, 16, LANES), jnp.bfloat16),
            pltpu.VMEM((N_TM, PAIRS, 2, 8, LANES), jnp.float32),
            pltpu.VMEM((N_TM, PAIRS, 2, 8, LANES), jnp.float32),
            pltpu.VMEM((FIRST, 8, LANES), jnp.float32),
            pltpu.SemaphoreType.DMA,
            pltpu.SemaphoreType.DMA((2,)),
            pltpu.SemaphoreType.DMA((chunks,)),
            pltpu.SemaphoreType.DMA((chunks,)),
            pltpu.SemaphoreType.DMA((chunks,)),
            pltpu.SemaphoreType.DMA((chunks,)),
        ],
        compiler_params=pltpu.CompilerParams(
            collective_id=0, has_side_effects=True, vmem_limit_bytes=48 << 20
        ),
    )(sample_delays, fringe_rates, data)
    return vis.reshape(2, 4, STATIONS, LANES), auto


def solution(mesh):
    in_specs = (P(None, "stn", "tm"), P("stn"), P("stn"))
    out_specs = (P(None, "tm", None, "stn"), P("tm", "stn"))
    return jax.shard_map(
        per_device, mesh=mesh, in_specs=in_specs, out_specs=out_specs, check_vma=False
    )
```

```python
import functools
import math

import jax
import jax.numpy as jnp
from jax import lax
from jax.experimental import pallas as pl
from jax.experimental.pallas import tpu as pltpu
from jax.sharding import PartitionSpec as P

MESH = pl.DeviceIdType.MESH

LANES = 128
FIRST = 32
FRAMES_DEV = 128
STATIONS = 32
N_TM = 8
ROWS = 2 * FIRST * FRAMES_DEV
HALO = 32
TURN = 20
CHUNKS = (2, 4, 4, 3, 2, 1)
PAIRS = FIRST // 2
SIN = (1.0, -1 / 6, 1 / 120, -1 / 5040, 1 / 362880, -1 / 39916800, 1 / 6227020800)


def iota(shape, axis):
    return lax.broadcasted_iota(jnp.int32, shape, axis)


def cos_turns(phase):
    wrapped = phase & ((1 << TURN) - 1)
    folded = jnp.abs(wrapped - (1 << (TURN - 1)))
    w = (folded - (1 << (TURN - 2))).astype(jnp.float32) * (2.0 * math.pi / (1 << TURN))
    square = w * w
    total = jnp.full_like(w, SIN[-1])
    for coefficient in SIN[-2::-1]:
        total = total * square + coefficient
    return total * w


def sin_turns(phase):
    return cos_turns(phase - (1 << (TURN - 2)))


def nt_dot(left, right):
    return lax.dot_general(left, right, (((1,), (1,)), ((), ())), preferred_element_type=jnp.float32)


def kernel(
    delay_hbm, rate_hbm, x_ref, acc_ref,
    delay_ref, rate_ref, xb, first_ref, second_ref, perm_ref, twid_ref, frame_ref, turned_ref,
    tx, rx, rs_tx, rs_rx,
    scalar_sems, load_sems, halo_sems, tx_sems, rx_sems, rs_tx_sems, rs_rx_sems,
):
    me = lax.axis_index("stn")
    tm = lax.axis_index("tm")
    barrier = pltpu.get_barrier_semaphore()

    def greet_stn(k, carry):
        pl.semaphore_signal(barrier, inc=1, device_id={"stn": lax.rem(me + k, STATIONS)}, device_id_type=MESH)
        return carry

    def greet_tm(k, carry):
        pl.semaphore_signal(barrier, inc=1, device_id={"tm": lax.rem(tm + k, N_TM)}, device_id_type=MESH)
        return carry

    def load(piece):
        at = pl.multiple_of(piece * 1024, 1024)
        return pltpu.make_async_copy(x_ref.at[pl.ds(at, 1024)], xb.at[pl.ds(at, 1024)], load_sems.at[piece])

    scalars = [
        pltpu.make_async_copy(source, target, scalar_sems.at[i])
        for i, (source, target) in enumerate(((delay_hbm, delay_ref), (rate_hbm, rate_ref)))
    ]
    for copy in scalars:
        copy.start()
    for piece in range(8):
        load(piece).start()
    lax.fori_loop(1, STATIONS, greet_stn, 0)
    lax.fori_loop(1, N_TM, greet_tm, 0)

    xb[pl.ds(ROWS + HALO, 128 - HALO), :] = jnp.zeros((128 - HALO, LANES), jnp.bfloat16)

    @pl.when(tm == N_TM - 1)
    def _():
        xb[pl.ds(ROWS, HALO), :] = jnp.zeros((HALO, LANES), jnp.bfloat16)

    for copy in scalars:
        copy.wait()
    delay = delay_ref[0]
    rate = rate_ref[0]
    whole = delay >> 7
    part = delay & (LANES - 1)

    rows = iota((2 * FIRST, LANES), 0)
    lanes = iota((2 * FIRST, LANES), 1)
    k1 = rows & (FIRST - 1)
    for extra in range(2):
        shift = 2 * (whole + extra)
        j = ((lanes - shift) & 63) >> 1
        comp_in = lanes & 1
        comp_out = rows >> 5
        quarter = (comp_out - comp_in) * (1 << (TURN - 2))
        base = cos_turns(k1 * j * (1 << 15) + rate * 128 * j + quarter)
        base = base.reshape(2 * FIRST, 1, LANES)
        frame = iota((1, 8, LANES), 1)
        lane = iota((1, 8, LANES), 2)
        for v in range(5):
            hit = ((lane + (128 * v - shift)) >> 6) == frame
            block = jnp.where(hit, base, 0.0).reshape(2 * FIRST * 8, LANES)
            first_ref[:, pl.ds(extra * 640 + v * 128, 128)] = block.astype(jnp.bfloat16)

    k1 = iota((FIRST, LANES), 0)
    sample = (iota((FIRST, LANES), 1) - part) & (LANES - 1)
    phase = sample * k1 * 256 + rate * sample
    scale = 1.0 / 64.0
    twid_ref[0] = cos_turns(phase) * scale
    twid_ref[1] = sin_turns(phase) * scale
    start = tm * (FRAMES_DEV * 4096) + iota((FRAMES_DEV, LANES), 0) * 4096
    phase = rate * start
    frame_ref[0] = cos_turns(phase)
    frame_ref[1] = sin_turns(phase)

    row = iota((256, LANES), 0)
    sample = (iota((256, LANES), 1) - part) & (LANES - 1)
    k2 = (row >> 3) * 4 + (row & 3)
    phase = sample * k2 * (1 << 13)
    comp_out = (row >> 2) & 1
    for comp_in in range(2):
        quarter = (comp_out - comp_in) * (1 << (TURN - 2))
        second_ref[:, pl.ds(comp_in * LANES, LANES)] = cos_turns(phase + quarter).astype(jnp.bfloat16)

    out_row = iota((256, 256), 0)
    in_row = iota((256, 256), 1)
    channel = out_row >> 5
    source = (out_row & 15) * 16 + (channel >> 2) * 8 + ((out_row >> 4) & 1) * 4 + (channel & 3)
    perm_ref[...] = jnp.where(in_row == source, 1.0, 0.0).astype(jnp.bfloat16)

    def halo(target):
        return pltpu.make_async_remote_copy(
            src_ref=x_ref.at[pl.ds(0, HALO)],
            dst_ref=xb.at[pl.ds(ROWS, HALO)],
            send_sem=halo_sems.at[0],
            recv_sem=halo_sems.at[1],
            device_id={"tm": target},
            device_id_type=MESH,
        )

    lane_of = iota((1, 2 * LANES), 1) & (LANES - 1)
    upper = jnp.where(lane_of >= part, 1.0, 0.0).astype(jnp.bfloat16)
    lower = jnp.where(lane_of < part, 1.0, 0.0).astype(jnp.bfloat16)

    def first_stage(group, low, high):
        count = high - low
        base = pl.multiple_of(group * 1024, 1024)
        data = jnp.concatenate([xb[pl.ds(base, 640), :], xb[pl.ds(base + 512, 640), :]], axis=1)
        data = jnp.concatenate([data * upper, data * lower], axis=0)
        partial = [
            jnp.dot(first_ref[pl.ds(comp * 256 + 8 * low, 8 * count)], data, preferred_element_type=jnp.float32)
            for comp in range(2)
        ]
        tc = twid_ref[0, pl.ds(low, count)].reshape(count, 1, LANES)
        ts = twid_ref[1, pl.ds(low, count)].reshape(count, 1, LANES)
        parts = []
        for half in range(2):
            at = pl.multiple_of(group * 16 + half * 8, 8)
            pc = frame_ref[0, pl.ds(at, 8), :].reshape(1, 8, LANES)
            ps = frame_ref[1, pl.ds(at, 8), :].reshape(1, 8, LANES)
            wc = tc * pc - ts * ps
            ws = ts * pc + tc * ps
            real, imag = (p[:, half * 128 : half * 128 + 128].reshape(count, 8, LANES) for p in partial)
            parts.append((real * wc + imag * ws, imag * wc - real * ws))
        at = pl.multiple_of(group * 16, 16)
        for comp in range(2):
            both = jnp.concatenate([parts[0][comp], parts[1][comp]], axis=1)
            turned_ref[pl.ds(low, count), pl.ds(at, 16), pl.ds(comp * 128, 128)] = both.astype(jnp.bfloat16)

    head = 2 * CHUNKS[0]

    def head_group(group, carry):
        load(group + 1).wait()
        first_stage(group, 0, head)
        return carry

    def rest_group(group, carry):
        first_stage(group, head, FIRST)
        return carry

    load(0).wait()
    lax.fori_loop(0, 7, head_group, 0)

    pl.semaphore_wait(barrier, STATIONS - 1 + N_TM - 1)

    @pl.when(tm > 0)
    def _():
        halo(tm - 1).start()

    lax.fori_loop(0, 3, rest_group, 0)

    @pl.when(tm < N_TM - 1)
    def _():
        halo(tm).wait_recv()

    first_stage(7, 0, head)

    def second_stage(kp, carry):
        data = turned_ref[pl.ds(2 * kp, 2)].reshape(256, 256)
        spec = nt_dot(second_ref[...], data)
        even = spec[:, :128].reshape(32, 8, 128)
        odd = spec[:, 128:].reshape(32, 8, 128)
        tx[:, kp] = jnp.concatenate([even, odd], axis=1).astype(jnp.bfloat16)
        return carry

    def to_owner(at, count, index, owner):
        return pltpu.make_async_remote_copy(
            src_ref=tx.at[owner, pl.ds(at, count)],
            dst_ref=rx.at[me, pl.ds(at, count)],
            send_sem=tx_sems.at[index],
            recv_sem=rx_sems.at[index],
            device_id={"stn": owner},
            device_id_type=MESH,
        )

    def to_row_owner(at, count, index, owner):
        return pltpu.make_async_remote_copy(
            src_ref=rs_tx.at[owner, pl.ds(at, count)],
            dst_ref=rs_rx.at[tm, pl.ds(at, count)],
            send_sem=rs_tx_sems.at[index],
            recv_sem=rs_rx_sems.at[index],
            device_id={"tm": owner},
            device_id_type=MESH,
        )

    starts = [sum(CHUNKS[:i]) for i in range(len(CHUNKS))]
    for index, (at, count) in enumerate(zip(starts, CHUNKS)):
        if index == 1:
            lax.fori_loop(3, 8, rest_group, 0)
        lax.fori_loop(at, at + count, second_stage, 0)

        def send(k, carry, at=at, count=count, index=index):
            to_owner(at, count, index, lax.rem(me + k, STATIONS)).start()
            return carry

        lax.fori_loop(1, STATIONS, send, 0)
        pltpu.make_async_copy(
            tx.at[me, pl.ds(at, count)], rx.at[me, pl.ds(at, count)], rx_sems.at[index]
        ).start()

    lane_group = iota((1, LANES), 1) >> 5
    low_rows = iota((1, 8, LANES), 1) < 4

    def correlate(first, count):
        halves = []
        for half in range(2):
            data = [rx[pl.ds(16 * half, 16), first + i].reshape(256, LANES) for i in range(count)]
            moved = jnp.dot(perm_ref[...], jnp.concatenate(data, axis=1), preferred_element_type=jnp.float32)
            halves.append(moved.astype(jnp.bfloat16).reshape(8, 2, 16, 128 * count))
        for i in range(count):
            cut = slice(128 * i, 128 * i + 128)
            real = jnp.concatenate([halves[0][:, 0, :, cut], halves[1][:, 0, :, cut]], axis=1)
            imag = jnp.concatenate([halves[0][:, 1, :, cut], halves[1][:, 1, :, cut]], axis=1)
            plain = jnp.concatenate([real, imag], axis=2)
            crossed = jnp.concatenate([imag, -real], axis=2)
            both = jnp.concatenate([plain, crossed], axis=1)
            for quad in range(2):
                right = plain[4 * quad : 4 * quad + 4].reshape(128, 256)
                left = both[4 * quad : 4 * quad + 4].reshape(256, 256)
                product = nt_dot(left, right).reshape(4, 64, LANES)
                kept = product[0]
                for e in range(1, 4):
                    kept = jnp.where(lane_group == e, product[e], kept)
                kept = kept.reshape(2, 4, 8, LANES)
                turned = pltpu.roll(kept.reshape(8, 8, LANES), 4, 1).reshape(2, 4, 8, LANES)
                even = jnp.where(low_rows, kept[0], turned[1])
                odd = jnp.where(low_rows, turned[0], kept[1])
                mixed = jnp.concatenate([even.reshape(4, 1, 8, LANES), odd.reshape(4, 1, 8, LANES)], axis=1)
                rs_tx[:, first + i, quad] = mixed.reshape(N_TM, 8, LANES)


    def gather_sums(index):
        at, count = starts[index], CHUNKS[index]
        arrived = rs_rx.at[:, pl.ds(at, count)]
        pltpu.make_async_copy(arrived, arrived, rs_rx_sems.at[index]).wait()
        total = rs_rx[0, pl.ds(at, count)]
        for source in range(1, N_TM):
            total = total + rs_rx[source, pl.ds(at, count)]
        acc_ref[pl.ds(2 * at, 2 * count)] = total.reshape(2 * count, 8, LANES)

    for index, (at, count) in enumerate(zip(starts, CHUNKS)):
        arrived = rx.at[:, pl.ds(at, count)]
        pltpu.make_async_copy(arrived, arrived, rx_sems.at[index]).wait()

        def correlate_pair(pair, carry, at=at):
            correlate(at + 2 * pair, 2)
            return carry

        lax.fori_loop(0, count // 2, correlate_pair, 0)
        if count % 2:
            correlate(at + count - 1, 1)

        def send(k, carry, at=at, count=count, index=index):
            to_row_owner(at, count, index, lax.rem(tm + k, N_TM)).start()
            return carry

        lax.fori_loop(1, N_TM, send, 0)
        pltpu.make_async_copy(
            rs_tx.at[tm, pl.ds(at, count)], rs_rx.at[tm, pl.ds(at, count)], rs_rx_sems.at[index]
        ).start()
        if index > 0:
            gather_sums(index - 1)

    gather_sums(len(CHUNKS) - 1)

    for index, (at, count) in enumerate(zip(starts, CHUNKS)):
        sent = tx.at[pl.ds(0, STATIONS - 1), pl.ds(at, count)]
        pltpu.make_async_copy(sent, sent, tx_sems.at[index]).wait()
        sent = rs_tx.at[pl.ds(0, N_TM - 1), pl.ds(at, count)]
        pltpu.make_async_copy(sent, sent, rs_tx_sems.at[index]).wait()

    @pl.when(tm > 0)
    def _():
        halo(tm).wait_send()


def finish(acc_ref, vis_ref, auto_ref):
    tm = lax.axis_index("tm")
    lane_group = iota((32, LANES), 1) >> 5
    station = iota((32, LANES), 0)
    for comp in range(2):
        stacked = jnp.concatenate([acc_ref[:, 4 * comp + r, :] for r in range(4)], axis=0)
        flipped = stacked.T.reshape(4, 32, LANES)
        for r in range(4):
            block = jnp.zeros((32, LANES), jnp.float32)
            for k2 in range(4):
                shift = (32 * (k2 - r)) % 128
                piece = flipped[k2] if shift == 0 else pltpu.roll(flipped[k2], shift, 1)
                block = jnp.where(lane_group == k2, piece, block)
            diagonal = station == 4 * tm + r
            vis_ref[4 * comp + r] = jnp.where(diagonal, 0.0, block * (1.0 / 32.0))
            if comp == 0:
                own = jnp.sum(jnp.where(diagonal, block, 0.0), axis=0, keepdims=True)
                auto_ref[pl.ds(r, 1), :] = own * (1.0 / 1024.0)


def per_device(streams, sample_delays, fringe_rates):
    data = streams.reshape(2, ROWS // 2, LANES).transpose(1, 0, 2).reshape(ROWS, LANES)
    chunks = len(CHUNKS)
    sums = pl.pallas_call(
        kernel,
        out_shape=jax.ShapeDtypeStruct((FIRST, 8, LANES), jnp.float32),
        in_specs=[pl.BlockSpec(memory_space=pltpu.HBM)] * 3,
        out_specs=pl.BlockSpec(memory_space=pltpu.VMEM),
        scratch_shapes=[
            pltpu.SMEM((1,), jnp.int32),
            pltpu.SMEM((1,), jnp.int32),
            pltpu.VMEM((ROWS + 128, LANES), jnp.bfloat16),
            pltpu.VMEM((512, 1280), jnp.bfloat16),
            pltpu.VMEM((256, 256), jnp.bfloat16),
            pltpu.VMEM((256, 256), jnp.bfloat16),
            pltpu.VMEM((2, FIRST, LANES), jnp.float32),
            pltpu.VMEM((2, FRAMES_DEV, LANES), jnp.float32),
            pltpu.VMEM((FIRST, FRAMES_DEV, 256), jnp.bfloat16),
            pltpu.VMEM((STATIONS, PAIRS, 16, LANES), jnp.bfloat16),
            pltpu.VMEM((STATIONS, PAIRS, 16, LANES), jnp.bfloat16),
            pltpu.VMEM((N_TM, PAIRS, 2, 8, LANES), jnp.float32),
            pltpu.VMEM((N_TM, PAIRS, 2, 8, LANES), jnp.float32),
            pltpu.SemaphoreType.DMA((2,)),
            pltpu.SemaphoreType.DMA((8,)),
            pltpu.SemaphoreType.DMA((2,)),
            pltpu.SemaphoreType.DMA((chunks,)),
            pltpu.SemaphoreType.DMA((chunks,)),
            pltpu.SemaphoreType.DMA((chunks,)),
            pltpu.SemaphoreType.DMA((chunks,)),
        ],
        compiler_params=pltpu.CompilerParams(
            collective_id=0, has_side_effects=True, vmem_limit_bytes=52 << 20
        ),
    )(sample_delays, fringe_rates, data)
    vis, auto = pl.pallas_call(
        finish,
        out_shape=(
            jax.ShapeDtypeStruct((8, STATIONS, LANES), jnp.float32),
            jax.ShapeDtypeStruct((4, LANES), jnp.float32),
        ),
        compiler_params=pltpu.CompilerParams(vmem_limit_bytes=4 << 20),
    )(sums)
    return vis.reshape(2, 4, STATIONS, LANES), auto


def solution(mesh):
    in_specs = (P(None, "stn", "tm"), P("stn"), P("stn"))
    out_specs = (P(None, "tm", None, "stn"), P("tm", "stn"))
    return jax.shard_map(
        per_device, mesh=mesh, in_specs=in_specs, out_specs=out_specs, check_vma=False
    )
```

```python
import functools
import math

import jax
import jax.numpy as jnp
from jax import lax
from jax.experimental import pallas as pl
from jax.experimental.pallas import tpu as pltpu
from jax.sharding import PartitionSpec as P

MESH = pl.DeviceIdType.MESH

LANES = 128
FIRST = 32
FRAMES_DEV = 128
STATIONS = 32
N_TM = 8
ROWS = 2 * FIRST * FRAMES_DEV
HALO = 32
TURN = 20
HEAD_ROWS = 544
CHUNKS = (2, 4, 4, 3, 2, 1)
PAIRS = FIRST // 2
SIN = (1.0, -1 / 6, 1 / 120, -1 / 5040, 1 / 362880, -1 / 39916800, 1 / 6227020800)


def iota(shape, axis):
    return lax.broadcasted_iota(jnp.int32, shape, axis)


def cos_turns(phase):
    wrapped = phase & ((1 << TURN) - 1)
    folded = jnp.abs(wrapped - (1 << (TURN - 1)))
    w = (folded - (1 << (TURN - 2))).astype(jnp.float32) * (2.0 * math.pi / (1 << TURN))
    square = w * w
    total = jnp.full_like(w, SIN[-1])
    for coefficient in SIN[-2::-1]:
        total = total * square + coefficient
    return total * w


def sin_turns(phase):
    return cos_turns(phase - (1 << (TURN - 2)))


def nt_dot(left, right):
    return lax.dot_general(left, right, (((1,), (1,)), ((), ())), preferred_element_type=jnp.float32)


def kernel(
    delay_hbm, rate_hbm, x_ref, acc_ref,
    delay_ref, rate_ref, xb, first_ref, second_ref, perm_ref, twid_ref, frame_ref, turned_ref,
    tx, rx, rs_tx, rs_rx,
    scalar_sems, load_sems, halo_sems, tx_sems, rx_sems, rs_tx_sems, rs_rx_sems,
):
    me = lax.axis_index("stn")
    tm = lax.axis_index("tm")
    barrier = pltpu.get_barrier_semaphore()

    def greet_stn(k, carry):
        pl.semaphore_signal(barrier, inc=1, device_id={"stn": lax.rem(me + k, STATIONS)}, device_id_type=MESH)
        return carry

    def greet_tm(k, carry):
        pl.semaphore_signal(barrier, inc=1, device_id={"tm": lax.rem(tm + k, N_TM)}, device_id_type=MESH)
        return carry

    def load(piece):
        at = pl.multiple_of(piece * 1024, 1024)
        return pltpu.make_async_copy(x_ref.at[pl.ds(at, 1024)], xb.at[pl.ds(at, 1024)], load_sems.at[piece])

    scalars = [
        pltpu.make_async_copy(source, target, scalar_sems.at[i])
        for i, (source, target) in enumerate(((delay_hbm, delay_ref), (rate_hbm, rate_ref)))
    ]
    for copy in scalars:
        copy.start()
    for piece in range(8):
        load(piece).start()
    lax.fori_loop(1, STATIONS, greet_stn, 0, unroll=True)
    lax.fori_loop(1, N_TM, greet_tm, 0, unroll=True)

    xb[pl.ds(ROWS + HALO, 128 - HALO), :] = jnp.zeros((128 - HALO, LANES), jnp.bfloat16)

    @pl.when(tm == N_TM - 1)
    def _():
        xb[pl.ds(ROWS, HALO), :] = jnp.zeros((HALO, LANES), jnp.bfloat16)

    for copy in scalars:
        copy.wait()
    delay = delay_ref[0]
    rate = rate_ref[0]
    whole = delay >> 7
    part = delay & (LANES - 1)

    rows = iota((2 * FIRST, LANES), 0)
    lanes = iota((2 * FIRST, LANES), 1)
    k1 = rows & (FIRST - 1)
    for extra in range(2):
        shift = 2 * (whole + extra)
        j = ((lanes - shift) & 63) >> 1
        comp_in = lanes & 1
        comp_out = rows >> 5
        quarter = (comp_out - comp_in) * (1 << (TURN - 2))
        base = cos_turns(k1 * j * (1 << 15) + rate * 128 * j + quarter)
        base = base.reshape(2 * FIRST, 1, LANES)
        frame = iota((1, 8, LANES), 1)
        lane = iota((1, 8, LANES), 2)
        for v in range(5):
            hit = ((lane + (128 * v - shift)) >> 6) == frame
            block = jnp.where(hit, base, 0.0).reshape(2 * FIRST * 8, LANES)
            first_ref[:, pl.ds(extra * 640 + v * 128, 128)] = block.astype(jnp.bfloat16)

    k1 = iota((FIRST, LANES), 0)
    sample = (iota((FIRST, LANES), 1) - part) & (LANES - 1)
    phase = sample * k1 * 256 + rate * sample
    scale = 1.0 / 64.0
    twid_ref[0] = cos_turns(phase) * scale
    twid_ref[1] = sin_turns(phase) * scale
    start = tm * (FRAMES_DEV * 4096) + iota((FRAMES_DEV, LANES), 0) * 4096
    phase = rate * start
    frame_ref[0] = cos_turns(phase)
    frame_ref[1] = sin_turns(phase)

    row = iota((256, LANES), 0)
    sample = (iota((256, LANES), 1) - part) & (LANES - 1)
    k2 = (row >> 3) * 4 + (row & 3)
    phase = sample * k2 * (1 << 13)
    comp_out = (row >> 2) & 1
    for comp_in in range(2):
        quarter = (comp_out - comp_in) * (1 << (TURN - 2))
        second_ref[:, pl.ds(comp_in * LANES, LANES)] = cos_turns(phase + quarter).astype(jnp.bfloat16)

    out_row = iota((256, 256), 0)
    in_row = iota((256, 256), 1)
    channel = out_row >> 5
    source = (out_row & 15) * 16 + (channel >> 2) * 8 + ((out_row >> 4) & 1) * 4 + (channel & 3)
    perm_ref[...] = jnp.where(in_row == source, 1.0, 0.0).astype(jnp.bfloat16)

    def halo(target):
        return pltpu.make_async_remote_copy(
            src_ref=x_ref.at[pl.ds(0, HALO)],
            dst_ref=xb.at[pl.ds(ROWS, HALO)],
            send_sem=halo_sems.at[0],
            recv_sem=halo_sems.at[1],
            device_id={"tm": target},
            device_id_type=MESH,
        )

    lane_of = iota((1, 2 * LANES), 1) & (LANES - 1)
    upper = jnp.where(lane_of >= part, 1.0, 0.0).astype(jnp.bfloat16)
    wraps = lane_of < part
    lower = jnp.where(lane_of < part, 1.0, 0.0).astype(jnp.bfloat16)

    def first_stage(group, low, high):
        count = high - low
        base = pl.multiple_of(group * 1024, 1024)
        data = jnp.concatenate([xb[pl.ds(base, 640), :], xb[pl.ds(base + 512, 640), :]], axis=1)
        rows = [pl.ds(comp * 256 + 8 * low, 8 * count) for comp in range(2)]
        if low == 0:
            data = data[:HEAD_ROWS]
            table = [first_ref[rows[comp], pl.ds(640 * extra, HEAD_ROWS)] for extra in range(2) for comp in range(2)]
            product = jnp.dot(jnp.concatenate(table, axis=0), data, preferred_element_type=jnp.float32)
            product = product.reshape(4, 8 * count, 256)
            partial = [jnp.where(wraps, product[2 + comp], product[comp]) for comp in range(2)]
        else:
            data = jnp.concatenate([data * upper, data * lower], axis=0)
            partial = [jnp.dot(first_ref[rows[comp]], data, preferred_element_type=jnp.float32) for comp in range(2)]
        tc = twid_ref[0, pl.ds(low, count)].reshape(count, 1, LANES)
        ts = twid_ref[1, pl.ds(low, count)].reshape(count, 1, LANES)
        parts = []
        for half in range(2):
            at = pl.multiple_of(group * 16 + half * 8, 8)
            pc = frame_ref[0, pl.ds(at, 8), :].reshape(1, 8, LANES)
            ps = frame_ref[1, pl.ds(at, 8), :].reshape(1, 8, LANES)
            wc = tc * pc - ts * ps
            ws = ts * pc + tc * ps
            real, imag = (p[:, half * 128 : half * 128 + 128].reshape(count, 8, LANES) for p in partial)
            parts.append((real * wc + imag * ws, imag * wc - real * ws))
        at = pl.multiple_of(group * 16, 16)
        for comp in range(2):
            both = jnp.concatenate([parts[0][comp], parts[1][comp]], axis=1)
            turned_ref[pl.ds(low, count), pl.ds(at, 16), pl.ds(comp * 128, 128)] = both.astype(jnp.bfloat16)

    head = 2 * CHUNKS[0]

    def head_group(group, carry):
        load(group + 1).wait()
        first_stage(group, 0, head)
        return carry

    def rest_group(group, carry):
        first_stage(group, head, FIRST)
        return carry

    load(0).wait()
    lax.fori_loop(0, 7, head_group, 0)

    pl.semaphore_wait(barrier, STATIONS - 1 + N_TM - 1)

    @pl.when(tm > 0)
    def _():
        halo(tm - 1).start()

    @pl.when(tm < N_TM - 1)
    def _():
        halo(tm).wait_recv()

    first_stage(7, 0, head)

    def second_stage(first, count):
        data = turned_ref[pl.ds(2 * first, 2 * count)].reshape(256 * count, 256)
        spec = nt_dot(second_ref[...], data)
        for i in range(count):
            even = spec[:, 256 * i : 256 * i + 128].reshape(32, 8, 128)
            odd = spec[:, 256 * i + 128 : 256 * i + 256].reshape(32, 8, 128)
            tx[:, first + i] = jnp.concatenate([even, odd], axis=1).astype(jnp.bfloat16)

    def to_owner(at, count, index, owner):
        return pltpu.make_async_remote_copy(
            src_ref=tx.at[owner, pl.ds(at, count)],
            dst_ref=rx.at[me, pl.ds(at, count)],
            send_sem=tx_sems.at[index],
            recv_sem=rx_sems.at[index],
            device_id={"stn": owner},
            device_id_type=MESH,
        )

    def to_row_owner(at, count, index, owner):
        return pltpu.make_async_remote_copy(
            src_ref=rs_tx.at[owner, pl.ds(at, count)],
            dst_ref=rs_rx.at[tm, pl.ds(at, count)],
            send_sem=rs_tx_sems.at[index],
            recv_sem=rs_rx_sems.at[index],
            device_id={"tm": owner},
            device_id_type=MESH,
        )

    starts = [sum(CHUNKS[:i]) for i in range(len(CHUNKS))]
    for index, (at, count) in enumerate(zip(starts, CHUNKS)):
        if index == 1:
            lax.fori_loop(0, 8, rest_group, 0)

        def second_pair(pair, carry, at=at):
            second_stage(at + 2 * pair, 2)
            return carry

        lax.fori_loop(0, count // 2, second_pair, 0)
        if count % 2:
            second_stage(at + count - 1, 1)

        def send(k, carry, at=at, count=count, index=index):
            to_owner(at, count, index, lax.rem(me + k, STATIONS)).start()
            return carry

        lax.fori_loop(1, STATIONS, send, 0, unroll=True)
        pltpu.make_async_copy(
            tx.at[me, pl.ds(at, count)], rx.at[me, pl.ds(at, count)], rx_sems.at[index]
        ).start()

    lane_group = iota((1, LANES), 1) >> 5
    low_rows = iota((1, 8, LANES), 1) < 4

    def correlate(first, count):
        halves = []
        for half in range(2):
            data = [rx[pl.ds(16 * half, 16), first + i].reshape(256, LANES) for i in range(count)]
            moved = jnp.dot(perm_ref[...], jnp.concatenate(data, axis=1), preferred_element_type=jnp.float32)
            halves.append(moved.astype(jnp.bfloat16).reshape(8, 2, 16, 128 * count))
        for i in range(count):
            cut = slice(128 * i, 128 * i + 128)
            real = jnp.concatenate([halves[0][:, 0, :, cut], halves[1][:, 0, :, cut]], axis=1)
            imag = jnp.concatenate([halves[0][:, 1, :, cut], halves[1][:, 1, :, cut]], axis=1)
            plain = jnp.concatenate([real, imag], axis=2)
            crossed = jnp.concatenate([imag, -real], axis=2)
            both = jnp.concatenate([plain, crossed], axis=1)
            for quad in range(2):
                right = plain[4 * quad : 4 * quad + 4].reshape(128, 256)
                left = both[4 * quad : 4 * quad + 4].reshape(256, 256)
                product = nt_dot(left, right).reshape(4, 64, LANES)
                kept = product[0]
                for e in range(1, 4):
                    kept = jnp.where(lane_group == e, product[e], kept)
                kept = kept.reshape(2, 4, 8, LANES)
                turned = pltpu.roll(kept.reshape(8, 8, LANES), 4, 1).reshape(2, 4, 8, LANES)
                even = jnp.where(low_rows, kept[0], turned[1])
                odd = jnp.where(low_rows, turned[0], kept[1])
                mixed = jnp.concatenate([even.reshape(4, 1, 8, LANES), odd.reshape(4, 1, 8, LANES)], axis=1)
                rs_tx[:, first + i, quad] = mixed.reshape(N_TM, 8, LANES)


    def gather_sums(index):
        at, count = starts[index], CHUNKS[index]
        arrived = rs_rx.at[:, pl.ds(at, count)]
        pltpu.make_async_copy(arrived, arrived, rs_rx_sems.at[index]).wait()
        total = rs_rx[0, pl.ds(at, count)]
        for source in range(1, N_TM):
            total = total + rs_rx[source, pl.ds(at, count)]
        acc_ref[pl.ds(2 * at, 2 * count)] = total.reshape(2 * count, 8, LANES)

    for index, (at, count) in enumerate(zip(starts, CHUNKS)):
        arrived = rx.at[:, pl.ds(at, count)]
        pltpu.make_async_copy(arrived, arrived, rx_sems.at[index]).wait()

        def correlate_pair(pair, carry, at=at):
            correlate(at + 2 * pair, 2)
            return carry

        lax.fori_loop(0, count // 2, correlate_pair, 0)
        if count % 2:
            correlate(at + count - 1, 1)

        def send(k, carry, at=at, count=count, index=index):
            to_row_owner(at, count, index, lax.rem(tm + k, N_TM)).start()
            return carry

        for k in (4, 5, 3, 6, 2, 7, 1):
            send(k, 0)
        pltpu.make_async_copy(
            rs_tx.at[tm, pl.ds(at, count)], rs_rx.at[tm, pl.ds(at, count)], rs_rx_sems.at[index]
        ).start()
        if index > 0:
            gather_sums(index - 1)

    gather_sums(len(CHUNKS) - 1)

    for index, (at, count) in enumerate(zip(starts, CHUNKS)):
        sent = tx.at[pl.ds(0, STATIONS - 1), pl.ds(at, count)]
        pltpu.make_async_copy(sent, sent, tx_sems.at[index]).wait()
        sent = rs_tx.at[pl.ds(0, N_TM - 1), pl.ds(at, count)]
        pltpu.make_async_copy(sent, sent, rs_tx_sems.at[index]).wait()

    @pl.when(tm > 0)
    def _():
        halo(tm).wait_send()


def finish(acc_ref, vis_ref, auto_ref):
    tm = lax.axis_index("tm")
    lane_group = iota((32, LANES), 1) >> 5
    station = iota((32, LANES), 0)
    for comp in range(2):
        stacked = jnp.concatenate([acc_ref[:, 4 * comp + r, :] for r in range(4)], axis=0)
        flipped = stacked.T.reshape(4, 32, LANES)
        for r in range(4):
            block = jnp.zeros((32, LANES), jnp.float32)
            for k2 in range(4):
                shift = (32 * (k2 - r)) % 128
                piece = flipped[k2] if shift == 0 else pltpu.roll(flipped[k2], shift, 1)
                block = jnp.where(lane_group == k2, piece, block)
            diagonal = station == 4 * tm + r
            vis_ref[4 * comp + r] = jnp.where(diagonal, 0.0, block * (1.0 / 32.0))
            if comp == 0:
                own = jnp.sum(jnp.where(diagonal, block, 0.0), axis=0, keepdims=True)
                auto_ref[pl.ds(r, 1), :] = own * (1.0 / 1024.0)


def per_device(streams, sample_delays, fringe_rates):
    data = streams.reshape(2, ROWS // 2, LANES).transpose(1, 0, 2).reshape(ROWS, LANES)
    chunks = len(CHUNKS)
    sums = pl.pallas_call(
        kernel,
        out_shape=jax.ShapeDtypeStruct((FIRST, 8, LANES), jnp.float32),
        in_specs=[pl.BlockSpec(memory_space=pltpu.HBM)] * 3,
        out_specs=pl.BlockSpec(memory_space=pltpu.VMEM),
        scratch_shapes=[
            pltpu.SMEM((1,), jnp.int32),
            pltpu.SMEM((1,), jnp.int32),
            pltpu.VMEM((ROWS + 128, LANES), jnp.bfloat16),
            pltpu.VMEM((512, 1280), jnp.bfloat16),
            pltpu.VMEM((256, 256), jnp.bfloat16),
            pltpu.VMEM((256, 256), jnp.bfloat16),
            pltpu.VMEM((2, FIRST, LANES), jnp.float32),
            pltpu.VMEM((2, FRAMES_DEV, LANES), jnp.float32),
            pltpu.VMEM((FIRST, FRAMES_DEV, 256), jnp.bfloat16),
            pltpu.VMEM((STATIONS, PAIRS, 16, LANES), jnp.bfloat16),
            pltpu.VMEM((STATIONS, PAIRS, 16, LANES), jnp.bfloat16),
            pltpu.VMEM((N_TM, PAIRS, 2, 8, LANES), jnp.float32),
            pltpu.VMEM((N_TM, PAIRS, 2, 8, LANES), jnp.float32),
            pltpu.SemaphoreType.DMA((2,)),
            pltpu.SemaphoreType.DMA((8,)),
            pltpu.SemaphoreType.DMA((2,)),
            pltpu.SemaphoreType.DMA((chunks,)),
            pltpu.SemaphoreType.DMA((chunks,)),
            pltpu.SemaphoreType.DMA((chunks,)),
            pltpu.SemaphoreType.DMA((chunks,)),
        ],
        compiler_params=pltpu.CompilerParams(
            collective_id=0, has_side_effects=True, vmem_limit_bytes=52 << 20
        ),
    )(sample_delays, fringe_rates, data)
    vis, auto = pl.pallas_call(
        finish,
        out_shape=(
            jax.ShapeDtypeStruct((8, STATIONS, LANES), jnp.float32),
            jax.ShapeDtypeStruct((4, LANES), jnp.float32),
        ),
        compiler_params=pltpu.CompilerParams(vmem_limit_bytes=4 << 20),
    )(sums)
    return vis.reshape(2, 4, STATIONS, LANES), auto


def solution(mesh):
    in_specs = (P(None, "stn", "tm"), P("stn"), P("stn"))
    out_specs = (P(None, "tm", None, "stn"), P("tm", "stn"))
    return jax.shard_map(
        per_device, mesh=mesh, in_specs=in_specs, out_specs=out_specs, check_vma=False
    )
```

```python
import functools
import math

import jax
import jax.numpy as jnp
from jax import lax
from jax.experimental import pallas as pl
from jax.experimental.pallas import tpu as pltpu
from jax.sharding import PartitionSpec as P

MESH = pl.DeviceIdType.MESH

LANES = 128
FIRST = 32
FRAMES_DEV = 128
STATIONS = 32
N_TM = 8
ROWS = 2 * FIRST * FRAMES_DEV
HALO = 32
TURN = 20
HEAD_ROWS = 544
CHUNKS = (2, 4, 4, 3, 2, 1)
PAIRS = FIRST // 2
SIN = (1.0, -1 / 6, 1 / 120, -1 / 5040, 1 / 362880, -1 / 39916800, 1 / 6227020800)


def iota(shape, axis):
    return lax.broadcasted_iota(jnp.int32, shape, axis)


def cos_turns(phase):
    wrapped = phase & ((1 << TURN) - 1)
    folded = jnp.abs(wrapped - (1 << (TURN - 1)))
    w = (folded - (1 << (TURN - 2))).astype(jnp.float32) * (2.0 * math.pi / (1 << TURN))
    square = w * w
    total = jnp.full_like(w, SIN[-1])
    for coefficient in SIN[-2::-1]:
        total = total * square + coefficient
    return total * w


def sin_turns(phase):
    return cos_turns(phase - (1 << (TURN - 2)))


def nt_dot(left, right):
    return lax.dot_general(left, right, (((1,), (1,)), ((), ())), preferred_element_type=jnp.float32)


def kernel(
    delay_hbm, rate_hbm, x_ref, acc_ref,
    delay_ref, rate_ref, xb, first_ref, second_ref, perm_ref, twid_ref, frame_ref, turned_ref,
    tx, rx, rs_tx, rs_rx,
    scalar_sems, load_sems, halo_sems, tx_sems, rx_sems, rs_tx_sems, rs_rx_sems,
):
    me = lax.axis_index("stn")
    tm = lax.axis_index("tm")
    barrier = pltpu.get_barrier_semaphore()

    def greet_stn(k, carry):
        pl.semaphore_signal(barrier, inc=1, device_id={"stn": lax.rem(me + k, STATIONS)}, device_id_type=MESH)
        return carry

    def greet_tm(k, carry):
        pl.semaphore_signal(barrier, inc=1, device_id={"tm": lax.rem(tm + k, N_TM)}, device_id_type=MESH)
        return carry

    def load(piece):
        at = pl.multiple_of(piece * 1024, 1024)
        return pltpu.make_async_copy(x_ref.at[pl.ds(at, 1024)], xb.at[pl.ds(at, 1024)], load_sems.at[piece])

    scalars = [
        pltpu.make_async_copy(source, target, scalar_sems.at[i])
        for i, (source, target) in enumerate(((delay_hbm, delay_ref), (rate_hbm, rate_ref)))
    ]
    for copy in scalars:
        copy.start()
    for piece in range(8):
        load(piece).start()
    lax.fori_loop(1, STATIONS, greet_stn, 0, unroll=True)
    lax.fori_loop(1, N_TM, greet_tm, 0, unroll=True)

    xb[pl.ds(ROWS + HALO, 128 - HALO), :] = jnp.zeros((128 - HALO, LANES), jnp.bfloat16)

    @pl.when(tm == N_TM - 1)
    def _():
        xb[pl.ds(ROWS, HALO), :] = jnp.zeros((HALO, LANES), jnp.bfloat16)

    for copy in scalars:
        copy.wait()
    delay = delay_ref[0]
    rate = rate_ref[0]
    whole = delay >> 7
    part = delay & (LANES - 1)

    rows = iota((2 * FIRST, LANES), 0)
    lanes = iota((2 * FIRST, LANES), 1)
    k1 = rows & (FIRST - 1)
    for extra in range(2):
        shift = 2 * (whole + extra)
        j = ((lanes - shift) & 63) >> 1
        comp_in = lanes & 1
        comp_out = rows >> 5
        quarter = (comp_out - comp_in) * (1 << (TURN - 2))
        base = cos_turns(k1 * j * (1 << 15) + rate * 128 * j + quarter)
        base = base.reshape(2 * FIRST, 1, LANES)
        frame = iota((1, 8, LANES), 1)
        lane = iota((1, 8, LANES), 2)
        for v in range(5):
            hit = ((lane + (128 * v - shift)) >> 6) == frame
            block = jnp.where(hit, base, 0.0).reshape(2 * FIRST * 8, LANES)
            first_ref[:, pl.ds(extra * 640 + v * 128, 128)] = block.astype(jnp.bfloat16)

    k1 = iota((FIRST, LANES), 0)
    sample = (iota((FIRST, LANES), 1) - part) & (LANES - 1)
    phase = sample * k1 * 256 + rate * sample
    scale = 1.0 / 64.0
    twid_ref[0] = cos_turns(phase) * scale
    twid_ref[1] = sin_turns(phase) * scale
    start = tm * (FRAMES_DEV * 4096) + iota((FRAMES_DEV, LANES), 0) * 4096
    phase = rate * start
    frame_ref[0] = cos_turns(phase)
    frame_ref[1] = sin_turns(phase)

    row = iota((256, LANES), 0)
    sample = (iota((256, LANES), 1) - part) & (LANES - 1)
    k2 = (row >> 3) * 4 + (row & 3)
    phase = sample * k2 * (1 << 13)
    comp_out = (row >> 2) & 1
    for comp_in in range(2):
        quarter = (comp_out - comp_in) * (1 << (TURN - 2))
        second_ref[:, pl.ds(comp_in * LANES, LANES)] = cos_turns(phase + quarter).astype(jnp.bfloat16)

    out_row = iota((256, 256), 0)
    in_row = iota((256, 256), 1)
    channel = out_row >> 5
    source = (out_row & 15) * 16 + (channel >> 2) * 8 + ((out_row >> 4) & 1) * 4 + (channel & 3)
    perm_ref[...] = jnp.where(in_row == source, 1.0, 0.0).astype(jnp.bfloat16)

    def halo(target):
        return pltpu.make_async_remote_copy(
            src_ref=x_ref.at[pl.ds(0, HALO)],
            dst_ref=xb.at[pl.ds(ROWS, HALO)],
            send_sem=halo_sems.at[0],
            recv_sem=halo_sems.at[1],
            device_id={"tm": target},
            device_id_type=MESH,
        )

    lane_of = iota((1, 2 * LANES), 1) & (LANES - 1)
    upper = jnp.where(lane_of >= part, 1.0, 0.0).astype(jnp.bfloat16)
    wraps = lane_of < part
    lower = jnp.where(lane_of < part, 1.0, 0.0).astype(jnp.bfloat16)

    def first_stage(group, low, high):
        count = high - low
        base = pl.multiple_of(group * 1024, 1024)
        data = jnp.concatenate([xb[pl.ds(base, 640), :], xb[pl.ds(base + 512, 640), :]], axis=1)
        rows = [pl.ds(comp * 256 + 8 * low, 8 * count) for comp in range(2)]
        if low == 0:
            data = data[:HEAD_ROWS]
            table = [first_ref[rows[comp], pl.ds(640 * extra, HEAD_ROWS)] for extra in range(2) for comp in range(2)]
            product = jnp.dot(jnp.concatenate(table, axis=0), data, preferred_element_type=jnp.float32)
            product = product.reshape(4, 8 * count, 256)
            partial = [jnp.where(wraps, product[2 + comp], product[comp]) for comp in range(2)]
        else:
            data = jnp.concatenate([data * upper, data * lower], axis=0)
            partial = [jnp.dot(first_ref[rows[comp]], data, preferred_element_type=jnp.float32) for comp in range(2)]
        tc = twid_ref[0, pl.ds(low, count)].reshape(count, 1, LANES)
        ts = twid_ref[1, pl.ds(low, count)].reshape(count, 1, LANES)
        parts = []
        for half in range(2):
            at = pl.multiple_of(group * 16 + half * 8, 8)
            pc = frame_ref[0, pl.ds(at, 8), :].reshape(1, 8, LANES)
            ps = frame_ref[1, pl.ds(at, 8), :].reshape(1, 8, LANES)
            wc = tc * pc - ts * ps
            ws = ts * pc + tc * ps
            real, imag = (p[:, half * 128 : half * 128 + 128].reshape(count, 8, LANES) for p in partial)
            parts.append((real * wc + imag * ws, imag * wc - real * ws))
        at = pl.multiple_of(group * 16, 16)
        for comp in range(2):
            both = jnp.concatenate([parts[0][comp], parts[1][comp]], axis=1)
            turned_ref[pl.ds(low, count), pl.ds(at, 16), pl.ds(comp * 128, 128)] = both.astype(jnp.bfloat16)

    head = 2 * CHUNKS[0]

    def head_group(group, carry):
        load(group + 1).wait()
        first_stage(group, 0, head)
        return carry

    def rest_group(group, carry):
        first_stage(group, head, FIRST)
        return carry

    load(0).wait()
    lax.fori_loop(0, 7, head_group, 0)

    pl.semaphore_wait(barrier, STATIONS - 1 + N_TM - 1)

    @pl.when(tm > 0)
    def _():
        halo(tm - 1).start()

    @pl.when(tm < N_TM - 1)
    def _():
        halo(tm).wait_recv()

    first_stage(7, 0, head)

    def second_stage(first, count):
        data = turned_ref[pl.ds(2 * first, 2 * count)].reshape(256 * count, 256)
        spec = nt_dot(second_ref[...], data)
        for i in range(count):
            even = spec[:, 256 * i : 256 * i + 128].reshape(32, 8, 128)
            odd = spec[:, 256 * i + 128 : 256 * i + 256].reshape(32, 8, 128)
            tx[:, first + i] = jnp.concatenate([even, odd], axis=1).astype(jnp.bfloat16)

    def to_owner(at, count, index, owner):
        return pltpu.make_async_remote_copy(
            src_ref=tx.at[owner, pl.ds(at, count)],
            dst_ref=rx.at[me, pl.ds(at, count)],
            send_sem=tx_sems.at[index],
            recv_sem=rx_sems.at[index],
            device_id={"stn": owner},
            device_id_type=MESH,
        )

    def to_row_owner(at, count, index, owner):
        return pltpu.make_async_remote_copy(
            src_ref=rs_tx.at[owner, pl.ds(at, count)],
            dst_ref=rs_rx.at[tm, pl.ds(at, count)],
            send_sem=rs_tx_sems.at[index],
            recv_sem=rs_rx_sems.at[index],
            device_id={"tm": owner},
            device_id_type=MESH,
        )

    starts = [sum(CHUNKS[:i]) for i in range(len(CHUNKS))]
    for index, (at, count) in enumerate(zip(starts, CHUNKS)):
        if index == 1:
            lax.fori_loop(0, 8, rest_group, 0)

        def second_pair(pair, carry, at=at):
            second_stage(at + 2 * pair, 2)
            return carry

        lax.fori_loop(0, count // 2, second_pair, 0)
        if count % 2:
            second_stage(at + count - 1, 1)

        def send(k, carry, at=at, count=count, index=index):
            to_owner(at, count, index, lax.rem(me + k, STATIONS)).start()
            return carry

        lax.fori_loop(1, STATIONS, send, 0, unroll=True)
        pltpu.make_async_copy(
            tx.at[me, pl.ds(at, count)], rx.at[me, pl.ds(at, count)], rx_sems.at[index]
        ).start()

    lane_group = iota((1, LANES), 1) >> 5
    low_rows = iota((1, 8, LANES), 1) < 4

    def correlate(first, count):
        halves = []
        for half in range(2):
            data = [rx[pl.ds(16 * half, 16), first + i].reshape(256, LANES) for i in range(count)]
            moved = jnp.dot(perm_ref[...], jnp.concatenate(data, axis=1), preferred_element_type=jnp.float32)
            halves.append(moved.astype(jnp.bfloat16).reshape(8, 2, 16, 128 * count))
        for i in range(count):
            cut = slice(128 * i, 128 * i + 128)
            real = jnp.concatenate([halves[0][:, 0, :, cut], halves[1][:, 0, :, cut]], axis=1)
            imag = jnp.concatenate([halves[0][:, 1, :, cut], halves[1][:, 1, :, cut]], axis=1)
            plain = jnp.concatenate([real, imag], axis=2)
            crossed = jnp.concatenate([imag, -real], axis=2)
            both = jnp.concatenate([plain, crossed], axis=1)
            rows = []
            for quad in range(2):
                right = plain[4 * quad : 4 * quad + 4].reshape(128, 256)
                left = both[4 * quad : 4 * quad + 4].reshape(256, 256)
                product = nt_dot(left, right).reshape(4, 64, LANES)
                kept = product[0]
                for e in range(1, 4):
                    kept = jnp.where(lane_group == e, product[e], kept)
                kept = kept.reshape(2, 4, 8, LANES)
                turned = pltpu.roll(kept.reshape(8, 8, LANES), 4, 1).reshape(2, 4, 8, LANES)
                even = jnp.where(low_rows, kept[0], turned[1])
                odd = jnp.where(low_rows, turned[0], kept[1])
                mixed = jnp.concatenate([even.reshape(4, 1, 8, LANES), odd.reshape(4, 1, 8, LANES)], axis=1)
                rows.append(mixed.reshape(N_TM, 8, LANES))
            rs_tx[:, first + i] = jnp.concatenate(rows, axis=1).astype(jnp.bfloat16)


    def gather_sums(index):
        at, count = starts[index], CHUNKS[index]
        arrived = rs_rx.at[:, pl.ds(at, count)]
        pltpu.make_async_copy(arrived, arrived, rs_rx_sems.at[index]).wait()
        total = rs_rx[0, pl.ds(at, count)].astype(jnp.float32)
        for source in range(1, N_TM):
            total = total + rs_rx[source, pl.ds(at, count)].astype(jnp.float32)
        acc_ref[pl.ds(2 * at, 2 * count)] = total.reshape(2 * count, 8, LANES)

    for index, (at, count) in enumerate(zip(starts, CHUNKS)):
        arrived = rx.at[:, pl.ds(at, count)]
        pltpu.make_async_copy(arrived, arrived, rx_sems.at[index]).wait()

        def correlate_pair(pair, carry, at=at):
            correlate(at + 2 * pair, 2)
            return carry

        lax.fori_loop(0, count // 2, correlate_pair, 0)
        if count % 2:
            correlate(at + count - 1, 1)

        def send(k, carry, at=at, count=count, index=index):
            to_row_owner(at, count, index, lax.rem(tm + k, N_TM)).start()
            return carry

        for k in (4, 5, 3, 6, 2, 7, 1):
            send(k, 0)
        pltpu.make_async_copy(
            rs_tx.at[tm, pl.ds(at, count)], rs_rx.at[tm, pl.ds(at, count)], rs_rx_sems.at[index]
        ).start()
        if index > 0:
            gather_sums(index - 1)

    gather_sums(len(CHUNKS) - 1)

    for index, (at, count) in enumerate(zip(starts, CHUNKS)):
        sent = tx.at[pl.ds(0, STATIONS - 1), pl.ds(at, count)]
        pltpu.make_async_copy(sent, sent, tx_sems.at[index]).wait()
        sent = rs_tx.at[pl.ds(0, N_TM - 1), pl.ds(at, count)]
        pltpu.make_async_copy(sent, sent, rs_tx_sems.at[index]).wait()

    @pl.when(tm > 0)
    def _():
        halo(tm).wait_send()


def finish(acc_ref, vis_ref, auto_ref):
    tm = lax.axis_index("tm")
    lane_group = iota((32, LANES), 1) >> 5
    station = iota((32, LANES), 0)
    for comp in range(2):
        stacked = jnp.concatenate([acc_ref[:, 4 * comp + r, :] for r in range(4)], axis=0)
        flipped = stacked.T.reshape(4, 32, LANES)
        for r in range(4):
            block = jnp.zeros((32, LANES), jnp.float32)
            for k2 in range(4):
                shift = (32 * (k2 - r)) % 128
                piece = flipped[k2] if shift == 0 else pltpu.roll(flipped[k2], shift, 1)
                block = jnp.where(lane_group == k2, piece, block)
            diagonal = station == 4 * tm + r
            vis_ref[4 * comp + r] = jnp.where(diagonal, 0.0, block * (1.0 / 32.0))
            if comp == 0:
                own = jnp.sum(jnp.where(diagonal, block, 0.0), axis=0, keepdims=True)
                auto_ref[pl.ds(r, 1), :] = own * (1.0 / 1024.0)


def per_device(streams, sample_delays, fringe_rates):
    data = streams.reshape(2, ROWS // 2, LANES).transpose(1, 0, 2).reshape(ROWS, LANES)
    chunks = len(CHUNKS)
    sums = pl.pallas_call(
        kernel,
        out_shape=jax.ShapeDtypeStruct((FIRST, 8, LANES), jnp.float32),
        in_specs=[pl.BlockSpec(memory_space=pltpu.HBM)] * 3,
        out_specs=pl.BlockSpec(memory_space=pltpu.VMEM),
        scratch_shapes=[
            pltpu.SMEM((1,), jnp.int32),
            pltpu.SMEM((1,), jnp.int32),
            pltpu.VMEM((ROWS + 128, LANES), jnp.bfloat16),
            pltpu.VMEM((512, 1280), jnp.bfloat16),
            pltpu.VMEM((256, 256), jnp.bfloat16),
            pltpu.VMEM((256, 256), jnp.bfloat16),
            pltpu.VMEM((2, FIRST, LANES), jnp.float32),
            pltpu.VMEM((2, FRAMES_DEV, LANES), jnp.float32),
            pltpu.VMEM((FIRST, FRAMES_DEV, 256), jnp.bfloat16),
            pltpu.VMEM((STATIONS, PAIRS, 16, LANES), jnp.bfloat16),
            pltpu.VMEM((STATIONS, PAIRS, 16, LANES), jnp.bfloat16),
            pltpu.VMEM((N_TM, PAIRS, 16, LANES), jnp.bfloat16),
            pltpu.VMEM((N_TM, PAIRS, 16, LANES), jnp.bfloat16),
            pltpu.SemaphoreType.DMA((2,)),
            pltpu.SemaphoreType.DMA((8,)),
            pltpu.SemaphoreType.DMA((2,)),
            pltpu.SemaphoreType.DMA((chunks,)),
            pltpu.SemaphoreType.DMA((chunks,)),
            pltpu.SemaphoreType.DMA((chunks,)),
            pltpu.SemaphoreType.DMA((chunks,)),
        ],
        compiler_params=pltpu.CompilerParams(
            collective_id=0, has_side_effects=True, vmem_limit_bytes=52 << 20
        ),
    )(sample_delays, fringe_rates, data)
    vis, auto = pl.pallas_call(
        finish,
        out_shape=(
            jax.ShapeDtypeStruct((8, STATIONS, LANES), jnp.float32),
            jax.ShapeDtypeStruct((4, LANES), jnp.float32),
        ),
        compiler_params=pltpu.CompilerParams(vmem_limit_bytes=4 << 20),
    )(sums)
    return vis.reshape(2, 4, STATIONS, LANES), auto


def solution(mesh):
    in_specs = (P(None, "stn", "tm"), P("stn"), P("stn"))
    out_specs = (P(None, "tm", None, "stn"), P("tm", "stn"))
    return jax.shard_map(
        per_device, mesh=mesh, in_specs=in_specs, out_specs=out_specs, check_vma=False
    )
```
